128 devices in a mesh: dp: 8 (over z, y_hi), tensor: 16 (over y_lo, x, core).
Axes of the slice: x: 4, y: 4 (y_hi: 2, y_lo: 2; y = y_hi * 2 + y_lo), z: 4, core: 2. Of those that a mesh axis runs over, the one named last changes fastest.
Arguments:
- inputs: bfloat16 [1024, 7424], P(('dp', 'tensor')), may hold values from -6 to 6
- grad_out: bfloat16 [1024, 7424], P(('dp', 'tensor')), may hold values from -6 to 6
- w_in: bfloat16 [7424, 29696], P('tensor', 'dp'), may hold values from -0.0625 to 0.0625
- w_out: bfloat16 [29696, 7424], P('dp', 'tensor'), may hold values from -0.03125 to 0.03125
Outputs:
- grad_x: bfloat16 [1024, 7424], P(('dp', 'tensor'))
- grad_w1: float32 [7424, 29696], P('tensor', 'dp')
- grad_w2: float32 [29696, 7424], P('dp', 'tensor')
The draws below stay inside these ranges and needn't reach their ends.
All inputs are finite; a program needn't handle non-finite values.
Results may differ from the reference program's by a relative error of at most 0.028.
Values may be sent and summed in bfloat16 or wider, within the bound.
No kernel may reach another device: no remote copies, remote signals or barrier semaphores. Data moves between devices by JAX's collectives and lax.ppermute only.
A program may use at most 128 MiB of HBM per device.

```python
import math
import jax
import jax.numpy as jnp
from jax import lax

D = 7424
FF = 29696
TOKENS = 1024
DT = 464
N_TENSOR = 16


def block_scale(rng, dims, pieces, smallest, top_value):
    gain, own = 1.0, jax.random.fold_in(rng, 6)
    for position, parts in pieces:
        steps = jnp.exp(jax.random.uniform(jax.random.fold_in(own, position), (parts,), jnp.float32, smallest / len(pieces), top_value / len(pieces)))
        gain = gain * jnp.repeat(steps, dims[position] // parts).reshape([-1 if axis == position else 1 for axis in range(len(dims))])
    return gain


def scatter_about(stream_key, extent, deviation, bound, cuts=(), kind=jnp.bfloat16):
    drawn = deviation * jax.random.normal(stream_key, extent, jnp.float32)
    if cuts:
        drawn = drawn * block_scale(stream_key, extent, cuts, -0.22, 0.18)
    return jnp.clip(drawn, -bound, bound).astype(kind)


def setup_inputs(seed: int = 0) -> dict:
    seeds = jax.random.split(jax.random.key(seed), 5)
    return {
        "inputs": scatter_about(seeds[0], (TOKENS, D), 1.0, 6.0, ((0, 128),)),
        "grad_out": scatter_about(seeds[1], (TOKENS, D), 1.0, 6.0, ((0, 128),)),
        "w_in": scatter_about(seeds[2], (D, FF), D ** -0.5, 0.0625, ((0, 16), (1, 8))),
        "w_out": scatter_about(seeds[3], (FF, D), FF ** -0.5, 0.03125, ((0, 8), (1, 16))),
    }


inv_root_two = 0.7071067811865476
inv_root_two_pi = 0.3989422804014327

def gelu_parts(hidden):
    normal_cdf = 0.5 * (1.0 + lax.erf(hidden * inv_root_two))
    return (hidden * normal_cdf, normal_cdf + hidden * jnp.exp(-0.5 * hidden * hidden) * inv_root_two_pi)

def reference(inputs, grad_out, w_in, w_out):

    def add_block(totals, block):
        start = (block * DT).astype(jnp.int32)
        x_cols = lax.dynamic_slice_in_dim(inputs, start, DT, 1)
        w_rows = lax.dynamic_slice_in_dim(w_in, start, DT, 0)
        g_cols = lax.dynamic_slice_in_dim(grad_out, start, DT, 1)
        o_cols = lax.dynamic_slice_in_dim(w_out, start, DT, 1)
        h_part = jnp.dot(x_cols, w_rows, preferred_element_type=jnp.float32)
        g_part = lax.dot_general(g_cols, o_cols, (((1,), (1,)), ((), ())), preferred_element_type=jnp.float32)
        h_part = lax.optimization_barrier(h_part.astype(jnp.bfloat16)).astype(jnp.float32)
        g_part = lax.optimization_barrier(g_part.astype(jnp.bfloat16)).astype(jnp.float32)
        return ((totals[0] + h_part, totals[1] + g_part), None)
    start_zero = jnp.zeros((inputs.shape[0], w_in.shape[1]), jnp.float32)
    (hidden, grad_act), _ = lax.scan(add_block, (start_zero, start_zero), jnp.arange(N_TENSOR, dtype=jnp.int32))
    act_full, slope = gelu_parts(hidden)
    act = act_full.astype(jnp.bfloat16)
    grad_hidden = (grad_act * slope).astype(jnp.bfloat16)
    factor = 1.0 / math.sqrt(inputs.shape[0])
    grad_w2 = jnp.dot(act.T, grad_out, preferred_element_type=jnp.float32) * factor
    grad_w1 = jnp.dot(inputs.T, grad_hidden, preferred_element_type=jnp.float32) * factor
    grad_x = jnp.dot(grad_hidden, w_in.T, preferred_element_type=jnp.float32).astype(jnp.bfloat16)
    return (grad_x, grad_w1, grad_w2)
```

```python
import functools
import math

import jax
import jax.numpy as jnp
from jax import lax
from jax.experimental import pallas as pl
from jax.experimental.pallas import tpu as pltpu
from jax.sharding import Mesh
from jax.sharding import PartitionSpec as P

inv_root_two = 0.7071067811865476
inv_root_two_pi = 0.3989422804014327
AXES = ("z", "yh", "y", "x", "core")
TILE = 128
SPLIT = 12
bf16, f32 = jnp.bfloat16, jnp.float32


def gelu_parts(hidden):
    normal_cdf = 0.5 * (1.0 + lax.erf(hidden * inv_root_two))
    return (
        hidden * normal_cdf,
        normal_cdf + hidden * jnp.exp(-0.5 * hidden * hidden) * inv_root_two_pi,
    )


def ring(axis, step):
    return lambda v: lax.ppermute(v, axis, [(i, (i + step) % 4) for i in range(4)])


def swap(axis):
    return lambda v: lax.ppermute(v, axis, [(0, 1), (1, 0)])


def x_links():
    return ring("x", 1), ring("x", -1), ring("x", 2), swap("y")


def z_links():
    return ring("z", 1), ring("z", -1), ring("z", 2), swap("yh")


def call(body, outs, operands, scratch=(), smem=0, cost=None):
    return pl.pallas_call(
        body,
        out_shape=[jax.ShapeDtypeStruct(s, d) for s, d in outs],
        in_specs=[
            pl.BlockSpec(memory_space=pltpu.SMEM if i < smem else pltpu.VMEM)
            for i in range(len(operands))
        ],
        out_specs=[pl.BlockSpec(memory_space=pltpu.VMEM) for _ in outs],
        scratch_shapes=list(scratch),
        compiler_params=pltpu.CompilerParams(vmem_limit_bytes=48 * 2**20),
        cost_estimate=cost,
    )(*operands)


def dot(left, right, dims):
    return lax.dot_general(left, right, (dims, ((), ())), preferred_element_type=f32)


def pairs(first, last, step):
    whole = (last - first) // 2
    if whole:
        pl.loop(0, whole)(lambda i: step(first + 2 * i, 2))
    if (last - first) % 2:
        step(last - 1, 1)


def product_body(nt, na, rows, transposed, order, *refs):
    pieces, (w_own, w_sib) = refs[:8], refs[8:10]
    own, sib, up, down, far, over, keep_a, keep_b, blocks = refs[10:]
    for k in range(8):
        blocks[k] = pieces[k][...]
    for k in range(8):
        at = order[k]
        own[k * rows : (k + 1) * rows, :] = blocks[at, 0]
        sib[k * rows : (k + 1) * rows, :] = blocks[at, 1]

    def multiply(tile, count):
        cols = pl.ds(pl.multiple_of(tile * TILE, TILE), count * TILE)
        if transposed:
            total = dot(own[...], w_own[cols, :], ((1,), (1,)))
            total += dot(sib[...], w_sib[cols, :], ((1,), (1,)))
        else:
            total = dot(own[...], w_own[:, cols], ((1,), (0,)))
            total += dot(sib[...], w_sib[:, cols], ((1,), (0,)))
        return total.astype(bf16).reshape(8, rows, count * TILE)

    def ring_first(tile, count):
        total = multiply(tile, count)
        for j in range(count):
            part = total[:, :, j * TILE : (j + 1) * TILE]
            for dy in range(2):
                for ref, dx in ((keep_a, 0), (up, 1), (far, 2), (down, 3)):
                    ref[tile + j, dy] = part[4 * dy + dx]

    def across_first(tile, count):
        total = multiply(tile, count)
        for j in range(count):
            part = total[:, :, j * TILE : (j + 1) * TILE]
            keep_b[tile + j - na] = part[:4]
            over[tile + j - na] = part[4:]

    pairs(0, na, ring_first)
    pairs(na, nt, across_first)


def product(order, pieces, w_own, w_sib, nt, na, transposed):
    rows, feats = pieces[0].shape[1:]
    nb = nt - na
    return call(
        functools.partial(product_body, nt, na, rows, transposed),
        [((8 * rows, feats), bf16)] * 2
        + [((na, 2, rows, TILE), bf16)] * 3
        + [((nb, 4, rows, TILE), bf16)]
        + [((na, 2, rows, TILE), bf16), ((nb, 4, rows, TILE), bf16)],
        [order, *pieces, w_own, w_sib],
        [pltpu.VMEM((8, 2, rows, feats), bf16)],
        smem=1,
        cost=pl.CostEstimate(
            flops=2 * 8 * rows * 2 * feats * nt * TILE,
            bytes_accessed=4 * feats * nt * TILE + 16 * rows * nt * TILE,
            transcendentals=0,
        ),
    )


def add(*terms):
    total = terms[0].astype(f32)
    for term in terms[1:]:
        total = total + term.astype(f32)
    return total


def middle_body(r, l, x, y, keep_a, keep_b, y2, sum_a, r2, l2, x2, sum_b):
    def ring_first(t):
        total = add(keep_a[t], r[t], l[t], x[t])
        sum_a[t] = total[0]
        y2[t] = total[1].astype(bf16)

    def across_first(t):
        total = add(keep_b[t], y[t])
        sum_b[t] = total[0]
        r2[t] = total[1].astype(bf16)
        x2[t] = total[2].astype(bf16)
        l2[t] = total[3].astype(bf16)

    pl.loop(0, keep_a.shape[0])(ring_first)
    pl.loop(0, keep_b.shape[0])(across_first)


def act_body(y, sum_a, r, l, x, sum_b, act, slope):
    na = sum_a.shape[0]

    def put(t, hidden):
        a, s = gelu_parts(hidden)
        act[t] = a.astype(bf16)
        slope[t] = s

    pl.loop(0, na)(lambda t: put(t, add(sum_a[t], y[t])))
    pl.loop(0, sum_b.shape[0])(lambda t: put(na + t, add(sum_b[t], r[t], l[t], x[t])))


def slope_body(y, sum_a, r, l, x, sum_b, slope, out):
    na = sum_a.shape[0]

    def put(t, grad_act):
        out[t] = (grad_act * slope[t]).astype(bf16)

    pl.loop(0, na)(lambda t: put(t, add(sum_a[t], y[t])))
    pl.loop(0, sum_b.shape[0])(lambda t: put(na + t, add(sum_b[t], r[t], l[t], x[t])))


def reduce_first(made):
    up, down, far, over = x_links()
    return up(made[2]), down(made[3]), far(made[4]), over(made[5]), made[6], made[7]


def reduce_second(state):
    up, down, far, over = x_links()
    na, _, rows, _ = state[4].shape
    nb = state[5].shape[0]
    a, b = (na, rows, TILE), (nb, rows, TILE)
    y2, sum_a, r2, l2, x2, sum_b = call(
        middle_body, [(a, bf16), (a, f32), (b, bf16), (b, bf16), (b, bf16), (b, f32)], state
    )
    return over(y2), sum_a, up(r2), down(l2), far(x2), sum_b


def gather_first(v):
    up, down, far, over = x_links()
    return v, up(v), down(v), far(v), over(v)


def pack_body(r, l, x, y, to_ring, to_over):
    na = to_ring.shape[0]
    to_ring[...] = y[:na]
    to_over[:, 0] = l[na:]
    to_over[:, 1] = x[na:]
    to_over[:, 2] = r[na:]


def gather_second(state, na):
    up, down, far, over = x_links()
    v, r, l, x, y = state
    nt, rows, _ = v.shape
    to_ring, to_over = call(
        pack_body, [((na, rows, TILE), bf16), ((nt - na, 3, rows, TILE), bf16)], (r, l, x, y)
    )
    return *state, up(to_ring), down(to_ring), far(to_ring), over(to_over)


def whole_body(v, r, l, x, y, r2, l2, x2, y2, out):
    na, rows = r2.shape[0], v.shape[1]
    for k, ref in enumerate((v, l, x, r, y)):
        out[:, k * rows : (k + 1) * rows, :] = ref[...]
    for k, ref in enumerate((l2, x2, r2)):
        at = slice((5 + k) * rows, (6 + k) * rows)
        out[:na, at, :] = ref[...]
        out[na:, at, :] = y2[:, k]


def gather_end(state):
    nt, rows, _ = state[0].shape
    return call(whole_body, [((nt, 8 * rows, TILE), bf16)], state)[0]


def input_grad_body(order, dh, w_own, w_sib, keep, up, down, far, total, blocks):
    nt, rows = dh.shape[0], dh.shape[1] // 8
    feats = w_own.shape[0]
    total[...] = jnp.zeros_like(total)

    def multiply(tile, count):
        cols = pl.ds(pl.multiple_of(tile * TILE, TILE), count * TILE)
        left = jnp.concatenate([dh[tile + j] for j in range(count)], axis=1)
        total[0] += dot(left, w_own[:, cols], ((1,), (1,)))
        total[1] += dot(left, w_sib[:, cols], ((1,), (1,)))

    pairs(0, nt, multiply)
    for k in range(8):
        for half in range(2):
            blocks[order[k], half] = total[half, k * rows : (k + 1) * rows, :].astype(bf16)
    for h in range(2):
        for ref, dz in ((keep, 0), (up, 1), (far, 2), (down, 3)):
            ref[h] = blocks[4 * h + dz]


def weight_grad_body(factor, left_own, left_sib, right_own, right_sib, out):
    nt = right_own.shape[0]

    def multiply(tile, count):
        cols = pl.ds(pl.multiple_of(tile * TILE, TILE), count * TILE)
        total = 0.0
        for left, right in ((left_own, right_own), (left_sib, right_sib)):
            v = jnp.concatenate([right[tile + j] for j in range(count)], axis=1)
            total += dot(left[...], v, ((0,), (0,)))
        out[:, cols] = total * factor

    pairs(0, nt, multiply)


def weight_grad_rows_body(factor, left_own, left_sib, right_own, right_sib, out):
    nt = left_own.shape[0]

    def multiply(tile, count):
        cols = pl.ds(pl.multiple_of(tile * TILE, TILE), count * TILE)
        total = 0.0
        for left, right in ((left_own, right_own), (left_sib, right_sib)):
            v = jnp.concatenate([left[tile + j] for j in range(count)], axis=1)
            total += dot(v, right[...], ((0,), (0,)))
        out[cols, :] = total * factor

    pairs(0, nt, multiply)


def sum_body(keep, r, l, x, kept, sent):
    kept[...] = add(keep[0], r[0], l[0], x[0])
    sent[...] = add(keep[1], r[1], l[1], x[1]).astype(bf16)


def per_device(inputs, grad_out, w_in, w_out):
    yi, xi, core = lax.axis_index("y"), lax.axis_index("x"), lax.axis_index("core")
    tokens, width = inputs.shape
    feats, hidden_width = w_in.shape
    nt, na = hidden_width // TILE, SPLIT
    cc = swap("core")

    def by_chip(v):
        v = v.reshape(tokens, 8, 2, feats).transpose(2, 1, 0, 3)
        return jnp.where(core == 0, v, v[::-1])

    sent = jnp.stack([by_chip(inputs), by_chip(grad_out)]).transpose(2, 0, 1, 3, 4)
    got = lax.all_to_all(sent, ("y", "x"), split_axis=0, concat_axis=0, tiled=True)
    got = got.transpose(1, 2, 0, 3, 4).reshape(2, 2, 8 * tokens, feats)
    w_in_sib = cc(w_in)
    w_out_sib = cc(w_out)

    def gather_dp(v):
        up, down, far, over = z_links()
        h = over(v)
        r, l, x = up(v), down(v), far(v)
        return v, l, x, r, h, down(h), far(h), up(h)

    order = jnp.stack(
        [((yi + dy) % 2) * 4 + (xi + dx) % 4 for dy in range(2) for dx in range(4)]
    ).astype(jnp.int32)
    made_h = product(order, gather_dp(got[0]), w_in, w_in_sib, nt, na, False)
    x_own, x_sib = made_h[:2]
    state_h = reduce_first(made_h)
    made_g = product(order, gather_dp(got[1]), w_out, w_out_sib, nt, na, True)
    g_own, g_sib = made_g[:2]
    state_g = reduce_first(made_g)

    state_h = reduce_second(state_h)
    state_g = reduce_second(state_g)
    rows = x_own.shape[0] // 8
    flat = (nt, rows, TILE)
    act, slope = call(act_body, [(flat, bf16), (flat, f32)], state_h)
    dh = call(slope_body, [(flat, bf16)], (*state_g, slope))[0]

    state_d = gather_first(dh)
    state_a = gather_first(act)
    state_d = gather_second(state_d, na)
    state_a = gather_second(state_a, na)
    dh_own = gather_end(state_d)
    block = ((2, 2, rows, feats), bf16)
    up, down, far, over = z_links()
    keep, to_up, to_down, to_far = call(
        input_grad_body,
        [block] * 4,
        (order, dh_own, w_in, w_in_sib),
        [pltpu.VMEM((2, 8 * rows, feats), f32), pltpu.VMEM((8, 2, rows, feats), bf16)],
        smem=1,
        cost=pl.CostEstimate(flops=2 * 8 * rows * 2 * feats * nt * TILE, bytes_accessed=2**23, transcendentals=0),
    )
    got_gx = up(to_up), down(to_down), far(to_far)
    factor = 1.0 / math.sqrt(2 * 8 * rows)
    cost = pl.CostEstimate(flops=4 * 8 * rows * feats * nt * TILE, bytes_accessed=2**24, transcendentals=0)
    sum_w1 = call(
        functools.partial(weight_grad_body, factor),
        [(w_in.shape, f32)],
        (x_own, cc(x_sib), dh_own, cc(dh_own)),
        cost=cost,
    )[0]
    kept, sent = call(
        sum_body, [((2, rows, feats), f32), ((2, rows, feats), bf16)], (keep, *got_gx)
    )
    gx = add(kept, over(sent)).astype(bf16)
    gx = gx.reshape(2, 8, tokens, feats).transpose(1, 0, 2, 3)
    gx = lax.all_to_all(gx, ("y", "x"), split_axis=0, concat_axis=0, tiled=True)
    gx = gx.transpose(2, 0, 1, 3)
    gx = jnp.where(core == 0, gx, gx[:, :, ::-1]).reshape(tokens, width)
    act_own = gather_end(state_a)
    sum_w2 = call(
        functools.partial(weight_grad_rows_body, factor),
        [(w_out.shape, f32)],
        (act_own, cc(act_own), g_own, cc(g_sib)),
        cost=cost,
    )[0]
    return gx, sum_w1, sum_w2


def solution(mesh):
    inner = Mesh(mesh.devices.reshape(4, 2, 2, 4, 2), AXES)
    dp, tensor = ("z", "yh"), ("y", "x", "core")
    placed = (P(dp + tensor, None), P(dp + tensor, None), P(tensor, dp), P(dp, tensor))
    return jax.shard_map(
        per_device,
        mesh=inner,
        in_specs=placed,
        out_specs=(P(dp + tensor, None), P(tensor, dp), P(dp, tensor)),
        check_vma=False,
    )
```

```python
import functools
import math

import jax
import jax.numpy as jnp
from jax import lax
from jax.experimental import pallas as pl
from jax.experimental.pallas import tpu as pltpu
from jax.sharding import Mesh
from jax.sharding import PartitionSpec as P

inv_root_two = 0.7071067811865476
inv_root_two_pi = 0.3989422804014327
AXES = ("z", "yh", "y", "x", "core")
TILE = 128
SPLIT_DH = 17
WIDTH = 4
bf16, f32 = jnp.bfloat16, jnp.float32


def gelu_parts(hidden):
    normal_cdf = 0.5 * (1.0 + lax.erf(hidden * inv_root_two))
    return (
        hidden * normal_cdf,
        normal_cdf + hidden * jnp.exp(-0.5 * hidden * hidden) * inv_root_two_pi,
    )


def ring(axis, step):
    return lambda v: lax.ppermute(v, axis, [(i, (i + step) % 4) for i in range(4)])


def swap(axis):
    return lambda v: lax.ppermute(v, axis, [(0, 1), (1, 0)])


def x_links():
    return ring("x", 1), ring("x", -1), ring("x", 2), swap("y")


def z_links():
    return ring("z", 1), ring("z", -1), ring("z", 2), swap("yh")


def padded(shape, dtype):
    *lead, rows, cols = shape
    return math.prod(lead) * -(-rows // 16) * 16 * -(-cols // TILE) * TILE * jnp.dtype(dtype).itemsize


def call(body, outs, operands, scratch=(), smem=0, after=(), sems=0, token=False, hbm=0, hbm_out=False):
    held = [padded(v.shape, v.dtype) for v in operands[smem : len(operands) - hbm]]
    held += [padded(s, d) for s, d in (*(() if hbm_out else outs), *scratch)]
    n, m, k = len(operands), len(after), len(outs)
    outs = [*outs, ((8, TILE), f32)] if token else outs

    def run(*refs):
        given, made = refs[:n], refs[n + m :]
        body(*given, *made[:k], *made[len(outs) :])
        if token:
            made[k][...] = jnp.zeros((8, TILE), f32)

    spaces = [pltpu.SMEM] * smem + [pltpu.VMEM] * (n - smem - hbm) + [pltpu.HBM] * hbm + [pl.ANY] * m
    return pl.pallas_call(
        run,
        out_shape=[jax.ShapeDtypeStruct(s, d) for s, d in outs],
        in_specs=[pl.BlockSpec(memory_space=space) for space in spaces],
        out_specs=[pl.BlockSpec(memory_space=pltpu.HBM if hbm_out and i < k else pltpu.VMEM) for i in range(len(outs))],
        scratch_shapes=[pltpu.VMEM(s, d) for s, d in scratch] + [pltpu.SemaphoreType.DMA(sems)] * bool(sems),
        compiler_params=pltpu.CompilerParams(vmem_limit_bytes=sum(held) + 4 * 2**20),
        cost_estimate=pl.CostEstimate(flops=0, bytes_accessed=sum(held), transcendentals=0),
    )(*operands, *after)


def dot(left, right, dims):
    return lax.dot_general(left, right, (dims, ((), ())), preferred_element_type=f32)


def groups(count, size, step):
    whole = count // size
    if whole:
        pl.loop(0, whole)(lambda i: step(size * i, size))
    if count % size:
        step(size * whole, count % size)


def held_until(arrays, after):
    n = len(arrays)
    return pl.pallas_call(
        lambda *refs: None,
        out_shape=[jax.ShapeDtypeStruct(v.shape, v.dtype) for v in arrays],
        in_specs=[pl.BlockSpec(memory_space=pl.ANY)] * (n + len(after)),
        out_specs=[pl.BlockSpec(memory_space=pl.ANY)] * n,
        input_output_aliases={i: i for i in range(n)},
    )(*arrays, *after)


class Streamed:
    def __init__(self, sources, targets, sems, width):
        self.pairs, self.sems, self.width = list(zip(sources, targets)), sems, width
        self.count = sources[0].shape[1] // TILE
        groups(self.count, width, self.start)

    def start(self, tile, count):
        for c in self.copies(tile, count):
            c.start()

    def copies(self, tile, count):
        cols = columns(tile, count)
        return [
            pltpu.make_async_copy(a.at[:, cols], b.at[:, cols], self.sems.at[i, tile // self.width])
            for i, (a, b) in enumerate(self.pairs)
        ]

    def wait(self, tile, count):
        for c in self.copies(tile, count):
            c.wait()


def columns(tile, count):
    return pl.ds(tile * TILE if isinstance(tile, int) else pl.multiple_of(tile * TILE, TILE), count * TILE)


def add(*terms):
    total = terms[0].astype(f32)
    for term in terms[1:]:
        total = total + term.astype(f32)
    return total


def spread_body(core, x, g, out):
    feats = out.shape[-1]
    first = core[0] == 0
    for i, ref in enumerate((x, g)):
        v = ref[...].astype(f32)
        for chip in range(8):
            even, odd = (v[:, (2 * chip + c) * feats : (2 * chip + c + 1) * feats] for c in range(2))
            out[chip, 2 * i] = jnp.where(first, even, odd).astype(bf16)
            out[chip, 2 * i + 1] = jnp.where(first, odd, even).astype(bf16)


def collect_body(got, x, g):
    for ref, first in ((x, 0), (g, 2)):
        for half in range(2):
            v = got[:, first + half].astype(f32)
            ref[half] = v.reshape(v.shape[0] * v.shape[1], v.shape[2]).astype(bf16)


def halves_body(x, x_across, g, r, l, far, x_both, g_ring):
    x_both[0] = x[...]
    x_both[1] = x_across[...]
    for dz, ref in enumerate((g, l, far, r)):
        g_ring[dz] = ref[...]


def gather_dp(x, g, after):
    up, down, far, over = z_links()
    x_both, g_ring = call(
        halves_body,
        [((2, *x.shape), bf16), ((4, *g.shape), bf16)],
        (x, over(x), g, up(g), down(g), far(g)),
        after=after,
    )
    return (x_both, down(x_both), far(x_both), up(x_both)), (g_ring, over(g_ring))


def product_body(ring_first, order, *refs):
    count = 4 if ring_first else 2
    pieces, sources, (own, sib) = refs[:count], refs[count : count + 2], refs[count + 2 : count + 4]
    *outs, blocks, w_own, w_sib, sems = refs[count + 4 :]
    weights = Streamed(sources, (w_own, w_sib), sems, WIDTH)
    rows = pieces[0].shape[2]
    for dz in range(4):
        for dyh in range(2):
            blocks[4 * dyh + dz] = pieces[dz][dyh] if ring_first else pieces[dyh][dz]
    for k in range(8):
        own[k * rows : (k + 1) * rows, :] = blocks[order[k], 0]
        sib[k * rows : (k + 1) * rows, :] = blocks[order[k], 1]

    def multiply(tile, count):
        cols = columns(tile, count)
        weights.wait(tile, count)
        total = dot(own[...], w_own[:, cols], ((1,), (0,)))
        total += dot(sib[...], w_sib[:, cols], ((1,), (0,)))
        total = total.astype(bf16).reshape(8, rows, count * TILE)
        for j in range(count):
            part = total[:, :, j * TILE : (j + 1) * TILE]
            if ring_first:
                for k, ref in enumerate(outs):
                    ref[tile + j] = part[k]
            else:
                for dy, ref in enumerate(outs):
                    ref[tile + j] = part[4 * dy : 4 * dy + 4]

    groups(outs[0].shape[0], WIDTH, multiply)


def product(order, pieces, w_own, w_sib, ring_first, after=()):
    rows, feats = pieces[0].shape[2:]
    nt = w_own.shape[1] // TILE
    outs = [((nt, rows, TILE), bf16)] * 8 if ring_first else [((nt, 4, rows, TILE), bf16)] * 2
    return call(
        functools.partial(product_body, ring_first),
        [((8 * rows, feats), bf16)] * 2 + outs,
        [order, *pieces, w_own, w_sib],
        [((8, 2, rows, feats), bf16)] + [(w_own.shape, bf16)] * 2,
        smem=1,
        after=after,
        hbm=2,
        sems=(2, -(-nt // WIDTH)),
    )


def tiles(count, step):
    pl.loop(0, count)(step)


def ring_forward_body(up_own, down_own, r, l, up, down):
    def step(t):
        up[t] = add(up_own[t], r[t]).astype(bf16)
        down[t] = add(down_own[t], l[t]).astype(bf16)

    tiles(up.shape[0], step)


def ring_sum_body(keep, keep_across, l_near, r_near, r_far, l_far, kept, sent):
    def step(t):
        kept[t] = add(keep[t], l_near[t], r_far[t])
        sent[t] = add(keep_across[t], r_near[t], l_far[t]).astype(bf16)

    tiles(keep.shape[0], step)


def across_sum_body(keep, y, kept, up, far, down):
    def step(t):
        total = add(keep[t], y[t])
        kept[t] = total[0]
        for dx, ref in ((1, up), (2, far), (3, down)):
            ref[t] = total[dx].astype(bf16)

    tiles(keep.shape[0], step)


def act_body(kept, y, act, slope):
    def step(t):
        a, s = gelu_parts(add(kept[t], y[t]))
        act[t] = a.astype(bf16)
        slope[t] = s

    tiles(act.shape[0], step)


def slope_body(kept, r, l, x, slope, out):
    def step(t):
        out[t] = (add(kept[t], r[t], l[t], x[t]) * slope[t]).astype(bf16)

    tiles(out.shape[0], step)


def gather_first(v):
    up, down, far, over = x_links()
    return v, over(v), up(v), down(v), far(v)


def pack_body(y, r, l, x, to_ring, to_over):
    na = to_ring.shape[0]
    to_ring[...] = y[:na]
    for k, ref in enumerate((l, x, r)):
        to_over[:, k] = ref[na:]


def gather_second(state, na):
    up, down, far, over = x_links()
    nt, rows, _ = state[0].shape
    outs = [((na, rows, TILE), bf16), ((nt - na, 3, rows, TILE), bf16)]
    to_ring, to_over = call(pack_body, outs, state[1:])
    return *state, over(to_over), up(to_ring), down(to_ring), far(to_ring)


def whole_body(v, y, r, l, x, y2, r2, l2, x2, a, a_across, out, pair):
    na = r2.shape[0]
    pair[:, 0] = a[...]
    pair[:, 1] = a_across[...]
    for k, ref in enumerate((v, l, x, r, y)):
        out[:, k] = ref[...]
    for k, ref in enumerate((l2, x2, r2)):
        out[:na, 5 + k] = ref[...]
    out[na:, 5:] = y2[...]


def gather_end(state, a, a_across):
    nt, rows, _ = state[0].shape
    whole, pair = call(
        whole_body,
        [((nt, 8, rows, TILE), bf16), ((nt, 2, rows, TILE), bf16)],
        (*state, a, a_across),
    )
    return whole, swap("core")(whole), pair


def forward_body(r, l, up, down):
    up[...] = r[:, 0]
    down[...] = l[:, 1]


def gather_ring(pair):
    up, down, _, _ = x_links()
    nt, _, rows, _ = pair.shape
    r, l = up(pair), down(pair)
    to_up, to_down = call(forward_body, [((nt, rows, TILE), bf16)] * 2, (r, l))
    return pair, l, r, up(to_up), down(to_down)


def token_rows(pieces, tile, count):
    wide = [pieces[0][tile + j] for j in range(count)]
    return jnp.concatenate([v.reshape(v.shape[0] * v.shape[1], TILE) for v in wide], axis=1)


def input_grad_body(order, whole, w_from_own, w_from_sib, out, total, w_own, w_sib, sems):
    weights = Streamed((w_from_own, w_from_sib), (w_own, w_sib), sems, WIDTH)
    nt, rows = whole.shape[0], whole.shape[2]
    total[...] = jnp.zeros_like(total)

    def multiply(tile, count):
        cols = columns(tile, count)
        left = token_rows([whole], tile, count)
        weights.wait(tile, count)
        total[0] += dot(left, w_own[:, cols], ((1,), (1,)))
        total[1] += dot(left, w_sib[:, cols], ((1,), (1,)))

    groups(nt, WIDTH, multiply)
    for k in range(8):
        for half in range(2):
            out[order[k], half] = total[half, k * rows : (k + 1) * rows, :].astype(bf16)


def pair_rows(pieces, tile, count):
    pair, l, r, x_near, x_far = pieces
    wide = []
    for j in range(count):
        t = tile + j
        parts = [pair[t, 0], l[t, 0], x_near[t], r[t, 0], pair[t, 1], l[t, 1], x_far[t], r[t, 1]]
        wide.append(jnp.concatenate(parts, axis=0))
    return jnp.concatenate(wide, axis=1)


def weight_grad_body(factor, width, rows_of, left, left_sib, *refs):
    *right, out, turned, held, sems = refs
    own, sib = right[: len(right) // 2], right[len(right) // 2 :]
    nt = own[0].shape[0]
    half = left.shape[0]
    turned[:, :half] = left[...].T
    turned[:, half:] = left_sib[...].T

    def copy(i, tile, count):
        cols = columns(tile, count)
        return pltpu.make_async_copy(held.at[:, cols], out.at[:, cols], sems.at[i])

    def multiply(i, tile, count):
        both = jnp.concatenate([rows_of(own, tile, count), rows_of(sib, tile, count)], axis=0)
        held[:, columns(tile, count)] = dot(turned[...], both, ((1,), (0,))) * factor
        copy(i, tile, count).start()

    whole = nt // width
    pl.loop(0, whole)(lambda i: multiply(i, width * i, width))
    if nt % width:
        multiply(whole, width * whole, nt % width)
    pl.loop(0, whole)(lambda i: copy(i, width * i, width).wait())
    if nt % width:
        copy(whole, width * whole, nt % width).wait()


def weight_grad(left, left_sib, own, sib, rows_of, after):
    nt, feats = own[0].shape[0], left.shape[1]
    width = 4
    factor = 1.0 / math.sqrt(2 * left.shape[0])
    shape = (feats, nt * TILE)
    return call(
        functools.partial(weight_grad_body, factor, width, rows_of),
        [(shape, f32)],
        (left, left_sib, *own, *sib),
        [((feats, 2 * left.shape[0]), bf16), (shape, f32)],
        sems=(-(-nt // width),),
        hbm_out=True,
        after=after,
        token=True,
    )


def dp_sum_body(got, out):
    chips, _, tokens, feats = out.shape
    for half in range(2):
        total = add(*(got[k, half] for k in range(8)))
        out[:, half] = total.reshape(chips, tokens, feats).astype(bf16)


def join_body(core, got, out):
    feats = got.shape[-1]
    first = core[0] == 0
    wide = []
    for chip in range(8):
        own, sib = got[chip, 0].astype(f32), got[chip, 1].astype(f32)
        wide += [jnp.where(first, own, sib), jnp.where(first, sib, own)]
    out[...] = jnp.concatenate(wide, axis=1).astype(bf16)


def per_device(inputs, grad_out, w_in, w_out):
    yi, xi, core = lax.axis_index("y"), lax.axis_index("x"), lax.axis_index("core")
    core = core.astype(jnp.int32).reshape(1)
    tokens, width = inputs.shape
    feats = w_in.shape[0]
    nt = w_in.shape[1] // TILE
    rows = 8 * tokens
    cc = swap("core")
    w_out = w_out.T
    w_in_sib, w_out_sib = cc(w_in), cc(w_out)

    spread = call(spread_body, [((8, 4, tokens, feats), bf16)], (core, inputs, grad_out), smem=1)[0]
    got = lax.all_to_all(spread, ("y", "x"), split_axis=0, concat_axis=0, tiled=True)
    x_mine, g_mine = call(collect_body, [((2, rows, feats), bf16)] * 2, (got,))

    zi, hi = lax.axis_index("z"), lax.axis_index("yh")
    order = jnp.stack(
        [((yi + dy) % 2) * 4 + (xi + dx) % 4 for dy in range(2) for dx in range(4)]
    ).astype(jnp.int32)
    x_all, g_all = gather_dp(x_mine, g_mine, (w_in_sib, w_out_sib))

    up, down, far, over = x_links()
    g_own, g_sib, keep_g, to_over = product(order, g_all, w_out, w_out_sib, False, x_all[1:])
    got_g = over(to_over)
    x_own, x_sib, *parts = product(order, x_all, w_in, w_in_sib, True, (keep_g,))
    r, l = up(parts[2]), down(parts[6])
    l_near, r_near = down(parts[3]), up(parts[5])
    one = (nt, rows, TILE)
    to_up, to_down = call(ring_forward_body, [(one, bf16)] * 2, (parts[1], parts[7], r, l))
    r_far, l_far = up(to_up), down(to_down)
    kept_g, to_up, to_far, to_down = call(
        across_sum_body, [(one, f32)] + [(one, bf16)] * 3, (keep_g, got_g)
    )
    got_g = up(to_up), down(to_down), far(to_far)
    swapped = cc(x_sib), cc(g_sib)
    kept, sent = call(
        ring_sum_body,
        [(one, f32), (one, bf16)],
        (parts[0], parts[4], l_near, r_near, r_far, l_far),
        after=(*swapped, kept_g),
    )
    act, slope = call(act_body, [(one, bf16), (one, f32)], (kept, over(sent)))
    act_across = over(act)
    dh = call(slope_body, [(one, bf16)], (kept_g, *got_g, slope), after=(act_across,))[0]

    state_d = gather_second(gather_first(dh), SPLIT_DH)
    dh_own, dh_sib, act_pair = gather_end(state_d, act, act_across)
    act_own = gather_ring(act_pair)

    place = ((order // 4 + hi) % 2 + 2 * ((order % 4 + zi) % 4)).astype(jnp.int32)
    gx, token_gx = call(
        input_grad_body,
        [((8, 2, rows, feats), bf16)],
        (place, dh_own, w_in, w_in_sib),
        [((2, 8 * rows, feats), f32)] + [(w_in.shape, bf16)] * 2,
        smem=1,
        token=True,
        hbm=2,
        sems=(2, -(-nt // WIDTH)),
    )
    gx = lax.all_to_all(gx, ("z", "yh"), split_axis=0, concat_axis=0, tiled=True)
    sum_w1, token = weight_grad(x_own, swapped[0], [dh_own], [dh_sib], token_rows, (token_gx,))
    gx, token = call(
        dp_sum_body, [((8, 2, tokens, feats), bf16)], (gx,), after=(token,), token=True
    )
    gx = lax.all_to_all(gx, ("y", "x"), split_axis=0, concat_axis=0, tiled=True)
    grad_x = call(join_body, [((tokens, width), bf16)], (core, gx), smem=1)[0]
    act_own = held_until(act_own, (token,))
    act_sib = [cc(p) for p in act_own]
    sum_w2, _ = weight_grad(g_own, swapped[1], act_own, act_sib, pair_rows, (token,))
    return grad_x, sum_w1, sum_w2.T


def solution(mesh):
    inner = Mesh(mesh.devices.reshape(4, 2, 2, 4, 2), AXES)
    dp, tensor = ("z", "yh"), ("y", "x", "core")
    placed = (P(dp + tensor, None), P(dp + tensor, None), P(tensor, dp), P(dp, tensor))
    return jax.shard_map(
        per_device,
        mesh=inner,
        in_specs=placed,
        out_specs=(P(dp + tensor, None), P(tensor, dp), P(dp, tensor)),
        check_vma=False,
    )
```

```python
import functools
import math

import jax
import jax.numpy as jnp
from jax import lax
from jax.experimental import pallas as pl
from jax.experimental.pallas import tpu as pltpu
from jax.sharding import Mesh
from jax.sharding import PartitionSpec as P

inv_root_two = 0.7071067811865476
inv_root_two_pi = 0.3989422804014327
AXES = ("z", "yh", "y", "x", "core")
TILE = 128
SPLIT_DH = 17
WIDTH = 4
WIDE = 8
bf16, f32 = jnp.bfloat16, jnp.float32


def gelu_parts(hidden):
    normal_cdf = 0.5 * (1.0 + lax.erf(hidden * inv_root_two))
    return (
        hidden * normal_cdf,
        normal_cdf + hidden * jnp.exp(-0.5 * hidden * hidden) * inv_root_two_pi,
    )


def ring(axis, step):
    return lambda v: lax.ppermute(v, axis, [(i, (i + step) % 4) for i in range(4)])


def swap(axis):
    return lambda v: lax.ppermute(v, axis, [(0, 1), (1, 0)])


def x_links():
    return ring("x", 1), ring("x", -1), ring("x", 2), swap("y")


def padded(shape, dtype):
    *lead, rows, cols = shape
    return math.prod(lead) * -(-rows // 16) * 16 * -(-cols // TILE) * TILE * jnp.dtype(dtype).itemsize


def call(body, outs, operands, scratch=(), smem=0, after=(), sems=(), token=False, hbm=0, hbm_out=False, light=False):
    held = [padded(v.shape, v.dtype) for v in operands[smem : len(operands) - hbm]]
    held += [padded(s, d) for s, d in (*(() if hbm_out else outs), *scratch)]
    n, m, k = len(operands), len(after), len(outs)
    outs = [*outs, ((8, TILE), f32)] if token else outs

    def run(*refs):
        given, made = refs[:n], refs[n + m :]
        body(*given, *made[:k], *made[len(outs) :])
        if token:
            made[k][...] = jnp.zeros((8, TILE), f32)

    spaces = [pltpu.SMEM] * smem + [pltpu.VMEM] * (n - smem - hbm) + [pltpu.HBM] * hbm + [pl.ANY] * m
    return pl.pallas_call(
        run,
        out_shape=[jax.ShapeDtypeStruct(s, d) for s, d in outs],
        in_specs=[pl.BlockSpec(memory_space=space) for space in spaces],
        out_specs=[pl.BlockSpec(memory_space=pltpu.HBM if hbm_out and i < k else pltpu.VMEM) for i in range(len(outs))],
        scratch_shapes=[pltpu.VMEM(s, d) for s, d in scratch] + [pltpu.SemaphoreType.DMA(v) for v in sems],
        compiler_params=pltpu.CompilerParams(vmem_limit_bytes=sum(held) + 4 * 2**20),
        cost_estimate=pl.CostEstimate(flops=0, bytes_accessed=0 if light else sum(held), transcendentals=0),
    )(*operands, *after)


def dot(left, right, dims):
    return lax.dot_general(left, right, (dims, ((), ())), preferred_element_type=f32)


def groups(count, size, step):
    whole = count // size
    if whole:
        pl.loop(0, whole)(lambda i: step(size * i, size))
    if count % size:
        step(size * whole, count % size)


def held_until(arrays, after):
    n = len(arrays)
    return pl.pallas_call(
        lambda *refs: None,
        out_shape=[jax.ShapeDtypeStruct(v.shape, v.dtype) for v in arrays],
        in_specs=[pl.BlockSpec(memory_space=pl.ANY)] * (n + len(after)),
        out_specs=[pl.BlockSpec(memory_space=pl.ANY)] * n,
        input_output_aliases={i: i for i in range(n)},
    )(*arrays, *after)


class Streamed:
    def __init__(self, sources, target, sems, width):
        self.feats, self.sems, self.width, self.target = sources[0].shape[0], sems, width, target
        self.sources, self.room = sources, target.shape[0] // 2
        self.count = sources[0].shape[1] // TILE
        groups(self.count, width, self.start)
        for i in range(2):
            rest = slice(i * self.room + self.feats, (i + 1) * self.room)
            target[rest, :] = jnp.zeros((self.room - self.feats, target.shape[1]), bf16)

    def copies(self, tile, count):
        cols = columns(tile, count)
        return [
            pltpu.make_async_copy(
                ref.at[:, cols],
                self.target.at[i * self.room : i * self.room + self.feats, cols],
                self.sems.at[i, tile // self.width],
            )
            for i, ref in enumerate(self.sources)
        ]

    def start(self, tile, count):
        for c in self.copies(tile, count):
            c.start()

    def wait(self, tile, count):
        for c in self.copies(tile, count):
            c.wait()


def roomy(feats):
    return -(-feats // 256) * 256


def columns(tile, count):
    return pl.ds(tile * TILE if isinstance(tile, int) else pl.multiple_of(tile * TILE, TILE), count * TILE)


def add(*terms):
    total = terms[0].astype(f32)
    for term in terms[1:]:
        total = total + term.astype(f32)
    return total


def spread_body(core, x, g, out):
    feats = out.shape[-1]
    first = core[0] == 0
    for i, ref in enumerate((g, x)):
        v = ref[...].astype(f32)
        for chip in range(8):
            even, odd = (v[:, (2 * chip + c) * feats : (2 * chip + c + 1) * feats] for c in range(2))
            own = jnp.where(first, even, odd).astype(bf16)
            sib = jnp.where(first, odd, even).astype(bf16)
            for group in range(8):
                out[8 * group + chip, 2 * i] = own
                out[8 * group + chip, 2 * i + 1] = sib


def exchange(v):
    return lax.all_to_all(v, ("z", "yh", "y", "x"), split_axis=0, concat_axis=0, tiled=True)


def product_body(ring_first, order, *refs):
    got, *sources, own, sib = refs[:5]
    *outs, left, weight, sems = refs[5:]
    weights = Streamed(sources, weight, sems, WIDTH)
    feats, room = own.shape[1], left.shape[1] // 2
    rows = own.shape[0] // 8
    left[...] = jnp.zeros_like(left)
    for k in range(8):
        at = slice(k * rows, (k + 1) * rows)
        for half, ref in enumerate((own, sib)):
            v = got[pl.ds(order[k] * 8, 8), half + 2 * ring_first].astype(f32).reshape(rows, feats).astype(bf16)
            ref[at, :] = v
            left[at, half * room : half * room + feats] = v

    def multiply(tile, count):
        cols = columns(tile, count)
        weights.wait(tile, count)
        total = dot(left[...], weight[:, cols], ((1,), (0,))).astype(bf16)
        total = total.reshape(8, rows, count * TILE)
        for j in range(count):
            part = total[:, :, j * TILE : (j + 1) * TILE]
            if ring_first:
                for k, ref in enumerate(outs):
                    ref[tile + j] = part[k]
            else:
                for dy, ref in enumerate(outs):
                    ref[tile + j] = part[4 * dy : 4 * dy + 4]

    groups(outs[0].shape[0], WIDTH, multiply)


def product(order, got, w_own, w_sib, ring_first, after=()):
    rows, feats = 8 * got.shape[2], got.shape[3]
    nt = w_own.shape[1] // TILE
    outs = [((nt, rows, TILE), bf16)] * 8 if ring_first else [((nt, 4, rows, TILE), bf16)] * 2
    return call(
        functools.partial(product_body, ring_first),
        [((8 * rows, feats), bf16)] * 2 + outs,
        [order, got, w_own, w_sib],
        [
            ((8 * rows, 2 * roomy(feats)), bf16),
            ((2 * roomy(feats), nt * TILE), bf16),
        ],
        smem=1,
        after=after,
        hbm=2,
        sems=((2, -(-nt // WIDTH)),),
    )


def tiles(count, step):
    pl.loop(0, count)(step)


def ring_forward_body(up_own, down_own, r, l, x, g, up, down, both):
    def step(t):
        up[t] = add(up_own[t], r[t]).astype(bf16)
        down[t] = add(down_own[t], l[t]).astype(bf16)

    tiles(up.shape[0], step)
    feats, room = x.shape[1], both.shape[1] // 2
    both[:, :feats] = x[...]
    both[:, room : room + feats] = g[...]


def ring_sum_body(keep, keep_across, l_near, r_near, r_far, l_far, kept, sent):
    def step(t):
        kept[t] = add(keep[t], l_near[t], r_far[t])
        sent[t] = add(keep_across[t], r_near[t], l_far[t]).astype(bf16)

    tiles(keep.shape[0], step)


def across_sum_body(keep, y, kept, up, far, down):
    def step(t):
        total = add(keep[t], y[t])
        kept[t] = total[0]
        for dx, ref in ((1, up), (2, far), (3, down)):
            ref[t] = total[dx].astype(bf16)

    tiles(keep.shape[0], step)


def act_body(kept, y, act, slope):
    def step(t):
        a, s = gelu_parts(add(kept[t], y[t]))
        act[t] = a.astype(bf16)
        slope[t] = s

    tiles(act.shape[0], step)


def slope_body(kept, r, l, x, slope, out):
    def step(t):
        out[t] = (add(kept[t], r[t], l[t], x[t]) * slope[t]).astype(bf16)

    tiles(out.shape[0], step)


def gather_first(v):
    up, down, far, over = x_links()
    return v, over(v), up(v), down(v), far(v)


def pack_body(y, r, l, x, a, a_across, to_ring, to_over, pair):
    na = to_ring.shape[0]
    to_ring[...] = y[:na]
    for k, ref in enumerate((l, x, r)):
        to_over[:, k] = ref[na:]
    pair[:, 0] = a[...]
    pair[:, 1] = a_across[...]


def gather_second(state, na, a, a_across, after):
    up, down, far, over = x_links()
    nt, rows, _ = state[0].shape
    to_ring, to_over, pair = call(
        pack_body,
        [((na, rows, TILE), bf16), ((nt - na, 3, rows, TILE), bf16), ((nt, 2, rows, TILE), bf16)],
        (*state[1:], a, a_across),
        after=after,
    )
    return (*state, over(to_over), up(to_ring), down(to_ring), far(to_ring)), pair


def whole_body(v, y, r, l, x, y2, r2, l2, x2, out):
    na = r2.shape[0]
    for k, ref in enumerate((v, l, x, r, y)):
        out[:, k] = ref[...]
    for k, ref in enumerate((l2, x2, r2)):
        out[:na, 5 + k] = ref[...]
    out[na:, 5:] = y2[...]


def gather_end(state):
    nt, rows, _ = state[0].shape
    whole = call(whole_body, [((nt, 8, rows, TILE), bf16)], state)[0]
    return whole, swap("core")(whole)


def forward_body(pair, r, l, up, down, near):
    up[...] = r[:, 0]
    down[...] = l[:, 1]
    for k, ref in enumerate((pair, l, r)):
        near[:, 2 * k : 2 * k + 2] = ref[...]


def gather_ring(pair, after):
    up, down, _, _ = x_links()
    nt, _, rows, _ = pair.shape
    r, l = up(pair), down(pair)
    to_up, to_down, near, token = call(
        forward_body,
        [((nt, rows, TILE), bf16)] * 2 + [((nt, 6, rows, TILE), bf16)],
        (pair, r, l),
        after=after,
        token=True,
    )
    return near, (up(to_up), down(to_down)), token


def token_rows(pieces, tile, count):
    wide = [pieces[0][tile + j] for j in range(count)]
    return jnp.concatenate([v.reshape(v.shape[0] * v.shape[1], TILE) for v in wide], axis=1)


def input_grad_body(order, whole, w_own, w_sib, out, total, weight, sems):
    weights = Streamed((w_own, w_sib), weight, sems, WIDE)
    nt, rows = whole.shape[0], whole.shape[2]
    (tokens, feats), room = out.shape[2:], weight.shape[0] // 2
    total[...] = jnp.zeros_like(total)

    def multiply(tile, count):
        cols = columns(tile, count)
        left = token_rows([whole], tile, count)
        weights.wait(tile, count)
        total[...] += dot(left, weight[:, cols], ((1,), (1,)))

    groups(nt, WIDE, multiply)
    for k in range(8):
        for half in range(2):
            v = total[k * rows : (k + 1) * rows, half * room : half * room + feats]
            out[pl.ds(order[k] * 8, 8), half] = v.reshape(8, tokens, feats).astype(bf16)


def pair_rows(pieces, tile, count):
    near, x_near, x_far = pieces
    wide = []
    for j in range(count):
        t = tile + j
        parts = [near[t, 0], near[t, 2], x_near[t], near[t, 4], near[t, 1], near[t, 3], x_far[t], near[t, 5]]
        wide.append(jnp.concatenate(parts, axis=0))
    return jnp.concatenate(wide, axis=1)


def transposed_body(x_own, g_own, sibs, x, g):
    (half, feats), room = x_own.shape, sibs.shape[1] // 2
    for i, (own, out) in enumerate(((x_own, x), (g_own, g))):
        out[:, :half] = own[...].T
        out[:, half:] = sibs[:, i * room : i * room + feats].T


def weight_grad_body(factor, width, rows_of, turned, *refs):
    n = (len(refs) - 4) // 2
    sources, out, right, (held, sems, in_sems) = refs[:n], refs[n], refs[n + 1 : 2 * n + 1], refs[2 * n + 1 :]
    own, sib = right[: n // 2], right[n // 2 :]
    nt = own[0].shape[0]

    def fetch(tile, count):
        part = pl.ds(tile, count)
        return [
            pltpu.make_async_copy(a.at[part], b.at[part], in_sems.at[i, tile // width])
            for i, (a, b) in enumerate(zip(sources, right))
        ]

    def start(tile, count):
        for c in fetch(tile, count):
            c.start()

    def copy(tile, count):
        cols = columns(tile, count)
        return pltpu.make_async_copy(held.at[:, cols], out.at[:, cols], sems.at[tile // width])

    def multiply(tile, count):
        for c in fetch(tile, count):
            c.wait()
        both = jnp.concatenate([rows_of(own, tile, count), rows_of(sib, tile, count)], axis=0)
        held[:, columns(tile, count)] = dot(turned[...], both, ((1,), (0,))) * factor
        copy(tile, count).start()

    groups(nt, width, start)
    groups(nt, width, multiply)
    groups(nt, width, lambda tile, count: copy(tile, count).wait())


def weight_grad(turned, own, sib, rows_of, after):
    nt, (feats, tokens) = own[0].shape[0], turned.shape
    factor = 1.0 / math.sqrt(tokens)
    shape = (feats, nt * TILE)
    right = (*own, *sib)
    steps = -(-nt // WIDTH)
    return call(
        functools.partial(weight_grad_body, factor, WIDTH, rows_of),
        [(shape, f32)],
        (turned, *right),
        [(v.shape, bf16) for v in right] + [(shape, f32)],
        hbm=len(right),
        sems=((steps,), (len(right), steps)),
        hbm_out=True,
        after=after,
        token=True,
        light=True,
    )


def join_body(core, got, out):
    first = core[0] == 0
    wide = []
    for chip in range(8):
        own, sib = (add(*(got[8 * group + chip, half] for group in range(8))) for half in range(2))
        wide += [jnp.where(first, own, sib), jnp.where(first, sib, own)]
    out[...] = jnp.concatenate(wide, axis=1).astype(bf16)


def per_device(inputs, grad_out, w_in, w_out):
    yi, xi, core = lax.axis_index("y"), lax.axis_index("x"), lax.axis_index("core")
    core = core.astype(jnp.int32).reshape(1)
    tokens, width = inputs.shape
    feats = w_in.shape[0]
    nt = w_in.shape[1] // TILE
    rows = 8 * tokens
    cc = swap("core")
    w_out = w_out.T
    w_in_sib, w_out_sib = cc(w_in), cc(w_out)

    order = jnp.stack(
        [((yi + dy) % 2) * 4 + (xi + dx) % 4 for dy in range(2) for dx in range(4)]
    ).astype(jnp.int32)
    both = call(
        spread_body, [((64, 4, tokens, feats), bf16)], (core, inputs, grad_out), smem=1
    )[0]
    both = exchange(both)

    up, down, far, over = x_links()
    g_own, g_sib, keep_g, to_over = product(order, both, w_out, w_out_sib, False)
    got_g = over(to_over)
    x_own, x_sib, *parts = product(order, both, w_in, w_in_sib, True, (keep_g,))
    r, l = up(parts[2]), down(parts[6])
    l_near, r_near = down(parts[3]), up(parts[5])
    one = (nt, rows, TILE)
    to_up, to_down, sibs = call(
        ring_forward_body,
        [(one, bf16)] * 2 + [((8 * rows, 2 * roomy(feats)), bf16)],
        (parts[1], parts[7], r, l, x_sib, g_sib),
    )
    r_far, l_far = up(to_up), down(to_down)
    kept_g, to_up, to_far, to_down = call(
        across_sum_body, [(one, f32)] + [(one, bf16)] * 3, (keep_g, got_g)
    )
    got_g = up(to_up), down(to_down), far(to_far)
    swapped = cc(sibs)
    kept, sent = call(
        ring_sum_body,
        [(one, f32), (one, bf16)],
        (parts[0], parts[4], l_near, r_near, r_far, l_far),
        after=(kept_g,),
    )
    act, slope = call(act_body, [(one, bf16), (one, f32)], (kept, over(sent)))
    act_across = over(act)
    dh = call(slope_body, [(one, bf16)], (kept_g, *got_g, slope), after=(act_across, swapped))[0]
    x_turned, g_turned = call(
        transposed_body, [((feats, 16 * rows), bf16)] * 2, (x_own, g_own, swapped)
    )
    state_d, act_pair = gather_second(
        gather_first(dh), SPLIT_DH, act, act_across, (x_turned, g_turned)
    )
    dh_own, dh_sib = gather_end(state_d)

    gx, token = call(
        input_grad_body,
        [((64, 2, tokens, feats), bf16)],
        (order, dh_own, w_in, w_in_sib),
        [((8 * rows, 2 * roomy(feats)), f32), ((2 * roomy(feats), nt * TILE), bf16)],
        smem=1,
        token=True,
        hbm=2,
        sems=((2, -(-nt // WIDE)),),
    )
    near, far, token_act = gather_ring(act_pair, (token,))
    gx = exchange(*held_until([gx], (token_act,)))
    sum_w1, token = weight_grad(x_turned, [dh_own], [dh_sib], token_rows, (token,))
    act_own = near, *far
    sum_w2, token = weight_grad(g_turned, act_own, [cc(v) for v in act_own], pair_rows, (token,))
    grad_x = call(
        join_body, [((tokens, width), bf16)], (core, gx), smem=1, after=(token,)
    )[0]
    return grad_x, sum_w1, sum_w2.T


def solution(mesh):
    inner = Mesh(mesh.devices.reshape(4, 2, 2, 4, 2), AXES)
    dp, tensor = ("z", "yh"), ("y", "x", "core")
    placed = (P(dp + tensor, None), P(dp + tensor, None), P(tensor, dp), P(dp, tensor))
    return jax.shard_map(
        per_device,
        mesh=inner,
        in_specs=placed,
        out_specs=(P(dp + tensor, None), P(tensor, dp), P(dp, tensor)),
        check_vma=False,
    )
```

```python
import functools
import math

import jax
import jax.numpy as jnp
from jax import lax
from jax.experimental import pallas as pl
from jax.experimental.pallas import tpu as pltpu
from jax.sharding import Mesh
from jax.sharding import PartitionSpec as P

inv_root_two = 0.7071067811865476
inv_root_two_pi = 0.3989422804014327
AXES = ("z", "yh", "y", "x", "core")
TILE = 128
SPLIT_DH = 14
MOVED = 5
WIDTH = 8
WIDE = 8
bf16, f32 = jnp.bfloat16, jnp.float32


def gelu_parts(hidden):
    normal_cdf = 0.5 * (1.0 + lax.erf(hidden * inv_root_two))
    return (
        hidden * normal_cdf,
        normal_cdf + hidden * jnp.exp(-0.5 * hidden * hidden) * inv_root_two_pi,
    )


def ring(axis, step):
    return lambda v: lax.ppermute(v, axis, [(i, (i + step) % 4) for i in range(4)])


def swap(axis):
    return lambda v: lax.ppermute(v, axis, [(0, 1), (1, 0)])


def x_links():
    return ring("x", 1), ring("x", -1), ring("x", 2), swap("y")


def padded(shape, dtype):
    *lead, rows, cols = shape
    return math.prod(lead) * -(-rows // 16) * 16 * -(-cols // TILE) * TILE * jnp.dtype(dtype).itemsize


def call(body, outs, operands, scratch=(), smem=0, after=(), sems=(), token=False, hbm=0, hbm_out=False, light=False):
    held = [padded(v.shape, v.dtype) for v in operands[smem : len(operands) - hbm]]
    held += [padded(s, d) for s, d in (*(() if hbm_out else outs), *scratch)]
    n, m, k = len(operands), len(after), len(outs)
    outs = [*outs, ((8, TILE), f32)] if token else outs

    def run(*refs):
        given, made = refs[:n], refs[n + m :]
        body(*given, *made[:k], *made[len(outs) :])
        if token:
            made[k][...] = jnp.zeros((8, TILE), f32)

    spaces = [pltpu.SMEM] * smem + [pltpu.VMEM] * (n - smem - hbm) + [pltpu.HBM] * hbm + [pl.ANY] * m
    return pl.pallas_call(
        run,
        out_shape=[jax.ShapeDtypeStruct(s, d) for s, d in outs],
        in_specs=[pl.BlockSpec(memory_space=space) for space in spaces],
        out_specs=[pl.BlockSpec(memory_space=pltpu.HBM if hbm_out and i < k else pltpu.VMEM) for i in range(len(outs))],
        scratch_shapes=[pltpu.VMEM(s, d) for s, d in scratch] + [pltpu.SemaphoreType.DMA(v) for v in sems],
        compiler_params=pltpu.CompilerParams(vmem_limit_bytes=sum(held) + 4 * 2**20),
        cost_estimate=pl.CostEstimate(flops=0, bytes_accessed=0 if light else sum(held), transcendentals=0),
    )(*operands, *after)


def dot(left, right, dims):
    return lax.dot_general(left, right, (dims, ((), ())), preferred_element_type=f32)


def groups(count, size, step):
    whole = count // size
    if whole:
        pl.loop(0, whole)(lambda i: step(size * i, size))
    if count % size:
        step(size * whole, count % size)


def held_until(arrays, after):
    n = len(arrays)
    return pl.pallas_call(
        lambda *refs: None,
        out_shape=[jax.ShapeDtypeStruct(v.shape, v.dtype) for v in arrays],
        in_specs=[pl.BlockSpec(memory_space=pl.ANY)] * (n + len(after)),
        out_specs=[pl.BlockSpec(memory_space=pl.ANY)] * n,
        input_output_aliases={i: i for i in range(n)},
    )(*arrays, *after)


class Streamed:
    def __init__(self, sources, target, sems, width):
        self.feats, self.sems, self.width, self.target = sources[0].shape[0], sems, width, target
        self.sources, self.room = sources, target.shape[0] // 2
        self.count = sources[0].shape[1] // TILE
        groups(self.count, width, self.start)
        for i in range(2):
            rest = slice(i * self.room + self.feats, (i + 1) * self.room)
            target[rest, :] = jnp.zeros((self.room - self.feats, target.shape[1]), bf16)

    def copies(self, tile, count):
        cols = columns(tile, count)
        return [
            pltpu.make_async_copy(
                ref.at[:, cols],
                self.target.at[i * self.room : i * self.room + self.feats, cols],
                self.sems.at[i, tile // self.width],
            )
            for i, ref in enumerate(self.sources)
        ]

    def start(self, tile, count):
        for c in self.copies(tile, count):
            c.start()

    def wait(self, tile, count):
        for c in self.copies(tile, count):
            c.wait()


def roomy(feats):
    return -(-feats // 256) * 256


def columns(tile, count):
    return pl.ds(tile * TILE if isinstance(tile, int) else pl.multiple_of(tile * TILE, TILE), count * TILE)


def add(*terms):
    total = terms[0].astype(f32)
    for term in terms[1:]:
        total = total + term.astype(f32)
    return total


def spread_body(core, x, g, out):
    feats = out.shape[-1]
    first = core[0] == 0
    for i, ref in enumerate((g, x)):
        v = ref[...].astype(f32)
        for chip in range(8):
            even, odd = (v[:, (2 * chip + c) * feats : (2 * chip + c + 1) * feats] for c in range(2))
            own = jnp.where(first, even, odd).astype(bf16)
            sib = jnp.where(first, odd, even).astype(bf16)
            for group in range(8):
                out[8 * group + chip, 2 * i] = own
                out[8 * group + chip, 2 * i + 1] = sib


def exchange(v):
    return lax.all_to_all(v, ("z", "yh", "y", "x"), split_axis=0, concat_axis=0, tiled=True)


def product_body(ring_first, moved, order, *refs):
    extra, refs = refs[:ring_first], refs[ring_first:]
    got, *sources, own, sib = refs[:5]
    *outs, left, weight, sems = refs[5:]
    weights = Streamed(sources, weight, sems, WIDTH)
    feats, room = own.shape[1], left.shape[1] // 2
    rows = own.shape[0] // 8
    left[...] = jnp.zeros_like(left)
    for k in range(8):
        at = slice(k * rows, (k + 1) * rows)
        for half, ref in enumerate((own, sib)):
            v = got[pl.ds(order[k] * 8, 8), half + 2 * ring_first].astype(f32).reshape(rows, feats).astype(bf16)
            ref[at, :] = v
            left[at, half * room : half * room + feats] = v

    def multiply(tile, count):
        cols = columns(tile, count)
        weights.wait(tile, count)
        total = dot(left[...], weight[:, cols], ((1,), (0,))).astype(bf16)
        total = total.reshape(8, rows, count * TILE)
        for j in range(count):
            part = total[:, :, j * TILE : (j + 1) * TILE]
            if ring_first:
                for k, ref in enumerate(outs):
                    ref[tile + j] = part[k]
            else:
                for dy in range(2):
                    outs[dy][tile + j] = part[4 * dy : 4 * dy + 4]

    if ring_first:
        groups(weights.count, WIDTH, multiply)
        for k, ref in enumerate(outs):
            ref[weights.count :] = extra[0][:, k]
    else:
        rest = weights.count - moved
        groups(rest, WIDTH, multiply)
        weights.wait(rest, moved)
        cols = slice(rest * TILE, weights.count * TILE)
        total = dot(left[...], weight[:, cols], ((1,), (0,))).astype(bf16)
        total = total.reshape(8, rows, moved * TILE)
        for j in range(moved):
            outs[2][j] = total[:, :, j * TILE : (j + 1) * TILE]


def product(order, got, w_own, w_sib, extra=(), after=()):
    rows, feats = 8 * got.shape[2], got.shape[3]
    nt = w_own.shape[1] // TILE
    if extra:
        outs = [((nt + MOVED, rows, TILE), bf16)] * 8
    else:
        outs = [((nt - MOVED, 4, rows, TILE), bf16)] * 2 + [((MOVED, 8, rows, TILE), bf16)]
    return call(
        functools.partial(product_body, len(extra), MOVED),
        [((8 * rows, feats), bf16)] * 2 + outs,
        [order, *extra, got, w_own, w_sib],
        [
            ((8 * rows, 2 * roomy(feats)), bf16),
            ((2 * roomy(feats), nt * TILE), bf16),
        ],
        smem=1,
        after=after,
        hbm=2,
        sems=((2, -(-nt // WIDTH)),),
    )


def tiles(count, step):
    pl.loop(0, count)(step)


def ring_forward_body(up_own, down_own, r, l, x, g, up, down, both):
    def step(t):
        up[t] = add(up_own[t], r[t]).astype(bf16)
        down[t] = add(down_own[t], l[t]).astype(bf16)

    tiles(up.shape[0], step)
    feats, room = x.shape[1], both.shape[1] // 2
    both[:, :feats] = x[...]
    both[:, room : room + feats] = g[...]


def ring_sum_body(keep, keep_across, l_near, r_near, r_far, l_far, kept, sent):
    def step(t):
        kept[t] = add(keep[t], l_near[t], r_far[t])
        sent[t] = add(keep_across[t], r_near[t], l_far[t]).astype(bf16)

    tiles(keep.shape[0], step)


def across_sum_body(keep, y, kept, up, far, down):
    def step(t):
        total = add(keep[t], y[t])
        kept[t] = total[0]
        for dx, ref in ((1, up), (2, far), (3, down)):
            ref[t] = total[dx].astype(bf16)

    tiles(keep.shape[0], step)


def act_body(kept, y, act, slope):
    def step(t):
        a, s = gelu_parts(add(kept[t], y[t]))
        act[t] = a.astype(bf16)
        slope[t] = s

    tiles(act.shape[0], step)


def slope_body(kept, r, l, x, kept_ring, y, slope, out):
    first = kept.shape[0]

    def step(t):
        out[t] = (add(kept[t], r[t], l[t], x[t]) * slope[t]).astype(bf16)

    def moved_step(i):
        t, at = first + i, out.shape[0] + i
        out[t] = (add(kept_ring[at], y[at]) * slope[t]).astype(bf16)

    tiles(first, step)
    tiles(out.shape[0] - first, moved_step)


def gather_first(v):
    up, down, far, over = x_links()
    return v, over(v), up(v), down(v), far(v)


def pack_body(y, r, l, x, a, a_across, to_ring, to_over, pair):
    na = to_ring.shape[0]
    to_ring[...] = y[:na]
    for k, ref in enumerate((l, x, r)):
        to_over[:, k] = ref[na:]
    pair[:, 0] = a[...]
    pair[:, 1] = a_across[...]


def gather_second(state, na, a, a_across, after):
    up, down, far, over = x_links()
    nt, rows, _ = state[0].shape
    to_ring, to_over, pair = call(
        pack_body,
        [((na, rows, TILE), bf16), ((nt - na, 3, rows, TILE), bf16), ((nt, 2, rows, TILE), bf16)],
        (*state[1:], a, a_across),
        after=after,
    )
    return (*state, over(to_over), up(to_ring), down(to_ring), far(to_ring)), pair


def whole_body(v, y, r, l, x, y2, r2, l2, x2, *outs):
    for out in outs:
        place_whole(v, y, r, l, x, y2, r2, l2, x2, out)


def place_whole(v, y, r, l, x, y2, r2, l2, x2, out):
    na = r2.shape[0]
    for k, ref in enumerate((v, l, x, r, y)):
        out[:, k] = ref[...]
    for k, ref in enumerate((l2, x2, r2)):
        out[:na, 5 + k] = ref[...]
    out[na:, 5:] = y2[...]


def gather_end(state):
    nt, rows, _ = state[0].shape
    now, later = call(whole_body, [((nt, 8, rows, TILE), bf16)] * 2, state)
    return now, later, swap("core")(later)


def forward_body(pair, r, l, up, down, near):
    up[...] = r[:, 0]
    down[...] = l[:, 1]
    for k, ref in enumerate((pair, l, r)):
        near[:, 2 * k : 2 * k + 2] = ref[...]


def gather_ring(pair, after):
    up, down, _, _ = x_links()
    nt, _, rows, _ = pair.shape
    r, l = up(pair), down(pair)
    to_up, to_down, near, token = call(
        forward_body,
        [((nt, rows, TILE), bf16)] * 2 + [((nt, 6, rows, TILE), bf16)],
        (pair, r, l),
        after=after,
        token=True,
    )
    return near, (up(to_up), down(to_down)), token


def token_rows(pieces, tile, count):
    wide = [pieces[0][tile + j] for j in range(count)]
    return jnp.concatenate([v.reshape(v.shape[0] * v.shape[1], TILE) for v in wide], axis=1)


def input_grad_body(order, whole, w_own, w_sib, out, total, weight, sems):
    weights = Streamed((w_own, w_sib), weight, sems, WIDE)
    nt, rows = whole.shape[0], whole.shape[2]
    (tokens, feats), room = out.shape[2:], weight.shape[0] // 2
    total[...] = jnp.zeros_like(total)

    def multiply(tile, count):
        cols = columns(tile, count)
        left = token_rows([whole], tile, count)
        weights.wait(tile, count)
        total[...] += dot(left, weight[:, cols], ((1,), (1,)))

    groups(nt, WIDE, multiply)
    for k in range(8):
        for half in range(2):
            v = total[k * rows : (k + 1) * rows, half * room : half * room + feats]
            out[pl.ds(order[k] * 8, 8), half] = v.reshape(8, tokens, feats).astype(bf16)


def pair_rows(pieces, tile, count):
    near, x_near, x_far = pieces
    wide = []
    for j in range(count):
        t = tile + j
        parts = [near[t, 0], near[t, 2], x_near[t], near[t, 4], near[t, 1], near[t, 3], x_far[t], near[t, 5]]
        wide.append(jnp.concatenate(parts, axis=0))
    return jnp.concatenate(wide, axis=1)


def transposed_body(x_own, g_own, sibs, x, g):
    (half, feats), room = x_own.shape, sibs.shape[1] // 2
    for i, (own, out) in enumerate(((x_own, x), (g_own, g))):
        out[:, :half] = own[...].T
        out[:, half:] = sibs[:, i * room : i * room + feats].T


def weight_grad_body(factor, width, rows_of, turned, *refs):
    n = (len(refs) - 4) // 2
    sources, out, right, (held, sems, in_sems) = refs[:n], refs[n], refs[n + 1 : 2 * n + 1], refs[2 * n + 1 :]
    own, sib = right[: n // 2], right[n // 2 :]
    nt = own[0].shape[0]

    def fetch(tile, count):
        part = pl.ds(tile, count)
        return [
            pltpu.make_async_copy(a.at[part], b.at[part], in_sems.at[i, tile // width])
            for i, (a, b) in enumerate(zip(sources, right))
        ]

    def start(tile, count):
        for c in fetch(tile, count):
            c.start()

    def copy(tile, count):
        cols = columns(tile, count)
        return pltpu.make_async_copy(held.at[:, cols], out.at[:, cols], sems.at[tile // width])

    def multiply(tile, count):
        for c in fetch(tile, count):
            c.wait()
        both = jnp.concatenate([rows_of(own, tile, count), rows_of(sib, tile, count)], axis=0)
        held[:, columns(tile, count)] = dot(turned[...], both, ((1,), (0,))) * factor
        copy(tile, count).start()

    groups(nt, width, start)
    groups(nt, width, multiply)
    groups(nt, width, lambda tile, count: copy(tile, count).wait())


def weight_grad(turned, own, sib, rows_of, after):
    nt, (feats, tokens) = own[0].shape[0], turned.shape
    factor = 1.0 / math.sqrt(tokens)
    shape = (feats, nt * TILE)
    right = (*own, *sib)
    steps = -(-nt // WIDTH)
    return call(
        functools.partial(weight_grad_body, factor, WIDTH, rows_of),
        [(shape, f32)],
        (turned, *right),
        [(v.shape, bf16) for v in right] + [(shape, f32)],
        hbm=len(right),
        sems=((steps,), (len(right), steps)),
        hbm_out=True,
        after=after,
        token=True,
        light=True,
    )


def join_body(core, got, out):
    first = core[0] == 0
    wide = []
    for chip in range(8):
        own, sib = (add(*(got[8 * group + chip, half] for group in range(8))) for half in range(2))
        wide += [jnp.where(first, own, sib), jnp.where(first, sib, own)]
    out[...] = jnp.concatenate(wide, axis=1).astype(bf16)


def per_device(inputs, grad_out, w_in, w_out):
    yi, xi, core = lax.axis_index("y"), lax.axis_index("x"), lax.axis_index("core")
    core = core.astype(jnp.int32).reshape(1)
    tokens, width = inputs.shape
    feats = w_in.shape[0]
    nt = w_in.shape[1] // TILE
    rows = 8 * tokens
    cc = swap("core")
    w_out = w_out.T
    w_in_sib, w_out_sib = cc(w_in), cc(w_out)

    order = jnp.stack(
        [((yi + dy) % 2) * 4 + (xi + dx) % 4 for dy in range(2) for dx in range(4)]
    ).astype(jnp.int32)
    both = call(
        spread_body, [((64, 4, tokens, feats), bf16)], (core, inputs, grad_out), smem=1
    )[0]
    both = exchange(both)

    up, down, far, over = x_links()
    g_own, g_sib, keep_g, to_over, moved = product(order, both, w_out, w_out_sib)
    got_g = over(to_over)
    x_own, x_sib, *parts = product(order, both, w_in, w_in_sib, (moved,), (keep_g,))
    r, l = up(parts[2]), down(parts[6])
    l_near, r_near = down(parts[3]), up(parts[5])
    one, more, less = ((n, rows, TILE) for n in (nt, nt + MOVED, nt - MOVED))
    to_up, to_down, sibs = call(
        ring_forward_body,
        [(more, bf16)] * 2 + [((8 * rows, 2 * roomy(feats)), bf16)],
        (parts[1], parts[7], r, l, x_sib, g_sib),
    )
    r_far, l_far = up(to_up), down(to_down)
    kept_g, to_up, to_far, to_down = call(
        across_sum_body, [(less, f32)] + [(less, bf16)] * 3, (keep_g, got_g)
    )
    got_g = up(to_up), down(to_down), far(to_far)
    swapped = cc(sibs)
    kept, sent = call(
        ring_sum_body,
        [(more, f32), (more, bf16)],
        (parts[0], parts[4], l_near, r_near, r_far, l_far),
        after=(kept_g,),
    )
    y = over(sent)
    act, slope = call(act_body, [(one, bf16), (one, f32)], (kept, y), after=got_g[:1])
    act_across = over(act)
    dh = call(slope_body, [(one, bf16)], (kept_g, *got_g, kept, y, slope), after=(swapped,))[0]
    x_turned, g_turned = call(
        transposed_body, [((feats, 16 * rows), bf16)] * 2, (x_own, g_own, swapped)
    )
    state_d, act_pair = gather_second(
        gather_first(dh), SPLIT_DH, act, act_across, (x_turned, g_turned)
    )
    dh_now, dh_own, dh_sib = gather_end(state_d)

    gx, token = call(
        input_grad_body,
        [((64, 2, tokens, feats), bf16)],
        (order, dh_now, w_in, w_in_sib),
        [((8 * rows, 2 * roomy(feats)), f32), ((2 * roomy(feats), nt * TILE), bf16)],
        smem=1,
        token=True,
        hbm=2,
        sems=((2, -(-nt // WIDE)),),
    )
    near, far, token_act = gather_ring(act_pair, (token,))
    gx = exchange(*held_until([gx], (token_act,)))
    sum_w1, token = weight_grad(x_turned, [dh_own], [dh_sib], token_rows, (token,))
    act_own = near, *far
    sum_w2, token = weight_grad(g_turned, act_own, [cc(v) for v in act_own], pair_rows, (token,))
    grad_x = call(
        join_body, [((tokens, width), bf16)], (core, gx), smem=1, after=(token,)
    )[0]
    return grad_x, sum_w1, sum_w2.T


def solution(mesh):
    inner = Mesh(mesh.devices.reshape(4, 2, 2, 4, 2), AXES)
    dp, tensor = ("z", "yh"), ("y", "x", "core")
    placed = (P(dp + tensor, None), P(dp + tensor, None), P(tensor, dp), P(dp, tensor))
    return jax.shard_map(
        per_device,
        mesh=inner,
        in_specs=placed,
        out_specs=(P(dp + tensor, None), P(tensor, dp), P(dp, tensor)),
        check_vma=False,
    )
```
